32 devices in a mesh: lines: 2 (over y), shots: 16 (over z, x, core).
Axes of the slice: x: 2, y: 2, z: 4, core: 2. Of those that a mesh axis runs over, the one named last changes fastest.
Arguments:
- records: bfloat16 [2048, 1024, 256], P(('lines', 'shots')), parts along dimension 0, may hold values from -6 to 6
- missing: int32 [256], P('lines'), parts along dimension 0, may hold values from 0 to 1023, as said below
- neighbours: int32 [256, 3], P('lines'), parts along dimension 0, may hold values from 0 to 1023, as said below
- weights: float32 [256, 3], P('lines'), parts along dimension 0, may hold values from 0.2 to 0.6
- freq_bins: int32 [8], replicated, may hold values from 1 to 127, as said below
Outputs:
- multiples: bfloat16 [2048, 1024, 256], P(('lines', 'shots')), parts along dimension 0
The draws below stay inside these ranges and needn't reach their ends.
There are 2 independent parts, one for each index of `lines`. The reference program is written for one: setup_inputs(seed, part) draws one part's arguments, and reference() takes and returns one part's arrays. A program takes and returns all parts, laid end to end along the dimension named above; an argument that names none is the same for every part. Nothing has to cross between parts.
Inputs may be any that keep to these rules, and one draw needn't show every extreme that they name: `missing`: distinct and ascending; any two missing shots lie 3 or more apart, and every shot within 2 of a missing shot is recorded. `neighbours`: row i names 3 distinct recorded shots, each within 2 of missing[i]. `freq_bins`: 8 distinct bins.
All inputs are finite; a program needn't handle non-finite values.
Results may differ from the reference program's by a relative error of at most 0.0079.
Values may be sent and summed in bfloat16 or wider, within the bound.
A program may use at most 192 MiB of HBM per device.

```python
import math
import jax
import jax.numpy as jnp
from jax import lax

SHOTS = 1024
SAMPLES = 256
REACH = 2
NEIGH = 3
NMISS = 128
NFREQ = 8


def missing_layout(key):
    slot_count = SHOTS // 4
    slot_order = jax.random.permutation(jax.random.fold_in(key, 101), slot_count - 2)[:NMISS] + 1
    chosen = jnp.sort(slot_order)
    offset = jax.random.randint(jax.random.fold_in(key, 102), (NMISS,), 2, 4)
    return (chosen * 4 + offset).astype(jnp.int32)


def draw_missing(key, part):
    return missing_layout(key)


def draw_neighbours(key, part):
    missing = missing_layout(key)
    offsets = jnp.concatenate([-jnp.arange(1, REACH + 1), jnp.arange(1, REACH + 1)]).astype(jnp.int32)
    scores = jax.random.randint(jax.random.fold_in(key, 103), (NMISS, 2 * REACH), 0, 4096) * (2 * REACH) + jnp.arange(2 * REACH)[None, :]
    picked = jnp.argsort(scores, axis=1)[:, :NEIGH]
    return (missing[:, None] + offsets[picked]).astype(jnp.int32)


def draw_freq_bins(key, part):
    middle = jax.random.permutation(jax.random.fold_in(key, 201), SAMPLES // 2 - 3)[:NFREQ - 2] + 2
    complete = jnp.concatenate([middle, jnp.array([1, SAMPLES // 2 - 1])])
    shuffle = jax.random.permutation(jax.random.fold_in(key, 202), NFREQ)
    return complete[shuffle].astype(jnp.int32)


def steps_of(own_key, dims, cuts, low, largest):
    factor_of, own = 1.0, jax.random.fold_in(own_key, 6)
    for dim, parts in cuts:
        heights = jnp.exp(jax.random.uniform(jax.random.fold_in(own, dim), (parts,), jnp.float32, low / len(cuts), largest / len(cuts)))
        factor_of = factor_of * jnp.repeat(heights, dims[dim] // parts).reshape([-1 if axis == dim else 1 for axis in range(len(dims))])
    return factor_of


def normal_values(key, extent, spread, reach, pieces=(), kind=jnp.bfloat16):
    values = spread * jax.random.normal(key, extent, jnp.float32)
    if pieces:
        values = values * steps_of(key, extent, pieces, -0.22, 0.18)
    return jnp.clip(values, -reach, reach).astype(kind)


def setup_inputs(seed: int = 0, part: int = 0) -> dict:
    arg_keys = jax.random.split(jax.random.key(seed), 6)
    part_keys = jax.random.split(jax.random.fold_in(arg_keys[5], part), 6)
    return {
        "records": normal_values(part_keys[0], (SHOTS, SHOTS, SAMPLES), 1.0, 6.0, ((0, 16),)),
        "missing": draw_missing(jax.random.fold_in(jax.random.fold_in(arg_keys[5], part), 71), part),
        "neighbours": draw_neighbours(jax.random.fold_in(jax.random.fold_in(arg_keys[5], part), 71), part),
        "weights": jnp.clip(jax.random.uniform(part_keys[3], (NMISS, NEIGH), jnp.float32, 0.2, 0.6), 0.2, 0.6),
        "freq_bins": draw_freq_bins(jax.random.fold_in(arg_keys[5], 71), part),
    }


def tables(freq_bins):
    sample_ids = jnp.arange(SAMPLES, dtype=jnp.int32)
    phases = freq_bins[None, :] * sample_ids[:, None] % SAMPLES
    angles = phases.astype(jnp.float32) * (2.0 * math.pi / SAMPLES)
    trig_pair = jnp.stack([jnp.cos(angles), -jnp.sin(angles)], axis=-1)
    forward = (trig_pair / math.sqrt(SAMPLES)).astype(jnp.bfloat16)
    inverse = (trig_pair * math.sqrt(2.0 / NFREQ)).astype(jnp.bfloat16)
    return (forward, inverse)

def product_plane(plane_pair):
    real_part = plane_pair[0].astype(jnp.float32)
    imag_part = plane_pair[1].astype(jnp.float32)
    left_side = jnp.concatenate([real_part, imag_part], axis=1)
    right_side = jnp.concatenate([jnp.concatenate([real_part, imag_part], axis=1), jnp.concatenate([-imag_part, real_part], axis=1)], axis=0)
    factor = -1.0 / math.sqrt(SHOTS)
    summed = jnp.dot(left_side, right_side, precision=lax.Precision.HIGHEST)
    return (summed * factor).astype(jnp.bfloat16)

def reference(records, missing, neighbours, weights, freq_bins):
    forward, inverse = tables(freq_bins)
    spectra = jnp.dot(records.reshape(SHOTS * SHOTS, SAMPLES), forward.reshape(SAMPLES, 2 * NFREQ), preferred_element_type=jnp.float32)
    spectra = spectra.astype(jnp.bfloat16).reshape(SHOTS, SHOTS, NFREQ, 2)
    filled_rows = jnp.zeros((NMISS, SHOTS, NFREQ, 2), jnp.float32)
    for slot_index in range(NEIGH):
        picked = spectra[neighbours[:, slot_index]].astype(jnp.float32)
        filled_rows = filled_rows + weights[:, slot_index][:, None, None, None] * picked
    filled = spectra.at[missing].set(filled_rows.astype(jnp.bfloat16))
    planes = jnp.transpose(filled, (2, 3, 0, 1))
    predicted = lax.map(product_plane, planes)
    stacked = jnp.transpose(predicted.reshape(NFREQ, SHOTS, 2, SHOTS), (1, 3, 0, 2))
    inverse_rows = jnp.transpose(inverse, (1, 2, 0)).reshape(2 * NFREQ, SAMPLES)
    multiples = jnp.dot(stacked.reshape(SHOTS * SHOTS, 2 * NFREQ), inverse_rows, preferred_element_type=jnp.float32)
    return multiples.astype(jnp.bfloat16).reshape(SHOTS, SHOTS, SAMPLES)
```

```python
import functools
import math

import jax
import jax.numpy as jnp
from jax import lax
from jax.experimental import pallas as pl
from jax.experimental.pallas import tpu as pltpu
from jax.sharding import PartitionSpec as P

SB = 16
MESH = pl.DeviceIdType.MESH


def tables(freq_bins, sample_count):
    bin_count = freq_bins.shape[0]
    sample_ids = jnp.arange(sample_count, dtype=jnp.int32)
    phases = freq_bins[:, None] * sample_ids[None, :] % sample_count
    angles = phases.astype(jnp.float32) * (2.0 * math.pi / sample_count)
    trig_pair = jnp.stack([jnp.cos(angles), -jnp.sin(angles)], axis=1)
    forward = (trig_pair / math.sqrt(sample_count)).astype(jnp.bfloat16)
    inverse = (trig_pair * math.sqrt(2.0 / bin_count)).astype(jnp.bfloat16)
    return (forward, inverse)


def fill_rows(missing, neighbours, weights, rows, cols):
    hit = missing[None, :] == rows.reshape(-1, 1)
    kept = jnp.logical_not(jnp.any(hit, axis=1)).reshape(rows.shape)
    out = jnp.where((rows == cols) & kept, 1.0, 0.0)
    for k in range(neighbours.shape[1]):
        w = jnp.sum(jnp.where(hit, weights[None, :, k], 0.0), axis=1).reshape(rows.shape)
        n = jnp.sum(jnp.where(hit, neighbours[None, :, k], 0), axis=1).reshape(rows.shape)
        out = out + jnp.where(n == cols, w, 0.0)
    return out.astype(jnp.bfloat16)


def row_mod(shape):
    return lax.broadcasted_iota(jnp.int32, shape, 0) % SB


def main_kernel(
    n, bins, rows, half, blocks,
    x_ref, base_ref, gb_ref, back_ref,
    send, recv, other, full, right, ret,
    send_sem, recv_sem, fsend, frecv, bsend, brecv, lsem,
):
    step = pl.program_id(0) * 2 + pl.program_id(1)
    sb, h = pl.program_id(0), pl.program_id(1)
    me = lax.axis_index("shots")
    member = me % 2
    mine = me // 2
    order = n * rows

    @pl.when(step == 0)
    def _():
        barrier = pltpu.get_barrier_semaphore()

        def greet(d, c):
            pl.semaphore_signal(
                barrier, inc=1, device_id={"shots": (me + d) % n}, device_id_type=MESH
            )
            return c

        lax.fori_loop(1, n, greet, 0)
        pl.semaphore_wait(barrier, n - 1)

    mod = row_mod((bins * 2 * SB, x_ref.shape[2]))
    base = base_ref[...]
    acc = jnp.zeros((bins * 2 * SB, half), jnp.float32)
    for s in range(SB):
        left = jnp.where(mod == s, base, jnp.zeros_like(base))
        acc = acc + lax.dot_general(
            left, x_ref[s], (((1,), (1,)), ((), ())), preferred_element_type=jnp.float32
        )
    at = pl.multiple_of(sb * SB, SB)
    send[:, h, :, pl.ds(at, SB), :] = acc.astype(jnp.bfloat16).reshape(bins, 2, SB, half)

    def out_copy(j, hh, sbb):
        a = pl.multiple_of(sbb * SB, SB)
        return pltpu.make_async_remote_copy(
            src_ref=send.at[j, hh, :, pl.ds(a, SB), :],
            dst_ref=recv.at[me, :, pl.ds(a, SB), :],
            send_sem=send_sem.at[j * 2 + hh, sbb],
            recv_sem=recv_sem.at[me, sbb],
            device_id={"shots": j * 2 + hh},
            device_id_type=MESH,
        )

    def start_out(d, c):
        j = (mine + d) % bins

        @pl.when(j * 2 + h != me)
        def _():
            out_copy(j, h, sb).start()

        return c

    lax.fori_loop(1, bins + 1, start_out, 0)

    @pl.when(h == member)
    def _():
        recv[me, :, pl.ds(at, SB), :] = send[mine, h, :, pl.ds(at, SB), :]

    @pl.when(step == 2 * blocks - 1)
    def _():
        sibling = mine * 2 + 1 - member

        def forward(p, sbb):
            a = pl.multiple_of(sbb * SB, SB)
            return pltpu.make_async_remote_copy(
                src_ref=recv.at[p, :, pl.ds(a, SB), :],
                dst_ref=other.at[p, :, pl.ds(a, SB), :],
                send_sem=fsend.at[p, sbb],
                recv_sem=frecv.at[p, sbb],
                device_id={"shots": sibling},
                device_id_type=MESH,
            )

        def arrive(i, c):
            sbb, p = i // n, (me + i) % n
            a = pl.multiple_of(sbb * SB, SB)

            @pl.when(p != me)
            def _():
                pltpu.make_async_remote_copy(
                    src_ref=recv.at[p, :, pl.ds(a, SB), :],
                    dst_ref=recv.at[p, :, pl.ds(a, SB), :],
                    send_sem=send_sem.at[p, sbb],
                    recv_sem=recv_sem.at[p, sbb],
                    device_id={"shots": sibling},
                    device_id_type=MESH,
                ).wait_recv()

            forward(p, sbb).start()
            return c

        lax.fori_loop(0, blocks * n, arrive, 0)

        def fill(src, keep):
            def one(b, c):
                first = jnp.minimum(jnp.maximum(2 * b - 1, 0), n - 4)
                g = gb_ref[b]
                at_row = pl.multiple_of(b * 2 * rows, 2 * rows)
                for ch in range(2):
                    piece = src[pl.ds(first, 4), ch].reshape(4 * rows, half)
                    val = jnp.dot(g, piece, preferred_element_type=jnp.float32)
                    keep(ch, at_row, val.astype(jnp.bfloat16))
                return c

            lax.fori_loop(0, n // 2, one, 0)

        def keep_own(ch, at_row, val):
            full[ch, member, pl.ds(at_row, 2 * rows), :] = val
            right[ch, pl.ds(at_row, 2 * rows), :] = val
            if ch == 1:
                right[2, pl.ds(at_row, 2 * rows), :] = -val

        def keep_other(ch, at_row, val):
            full[ch, 1 - member, pl.ds(at_row, 2 * rows), :] = val

        fill(recv, keep_own)

        def arrived(i, c):
            forward(i % n, i // n).wait()
            return c

        lax.fori_loop(0, blocks * n, arrived, 0)
        fill(other, keep_other)

        def back_copy(p):
            return pltpu.make_async_remote_copy(
                src_ref=ret.at[p],
                dst_ref=back_ref.at[me],
                send_sem=bsend.at[p],
                recv_sem=brecv.at[me],
                device_id={"shots": p},
                device_id_type=MESH,
            )

        own_back = pltpu.make_async_copy(ret.at[me], back_ref.at[me], lsem)
        factor = -1.0 / math.sqrt(order)
        groups = n // 4
        wide = 256

        def product(i, c):
            g = (me // 4 + groups // 2 + i) % groups
            at_row = pl.multiple_of(g * 4 * rows, 4 * rows)

            for col in range(0, half, wide):
                for ch in range(2):
                    out = None
                    for m in range(2):
                        for lc in range(2):
                            rc = (0 if lc == 0 else 2) if ch == 0 else (1 if lc == 0 else 0)
                            term = jnp.dot(
                                full[lc, m, pl.ds(at_row, 4 * rows), :],
                                right[rc, m * half:(m + 1) * half, col:col + wide],
                                preferred_element_type=jnp.float32,
                            )
                            out = term if out is None else out + term
                    ret[pl.ds(4 * g, 4), ch, :, col:col + wide] = (
                        (out * factor).astype(jnp.bfloat16).reshape(4, rows, wide)
                    )

            def post(q, c2):
                p = 4 * g + q

                @pl.when(p != me)
                def _():
                    back_copy(p).start()

                @pl.when(p == me)
                def _():
                    own_back.start()

                return c2

            lax.fori_loop(0, 4, post, 0)
            return c

        lax.fori_loop(0, groups, product, 0)
        own_back.wait()

        def sent(i, c):
            sbb, p = i // n, i % n

            @pl.when(p != me)
            def _():
                out_copy(p // 2, p % 2, sbb).wait_send()

            return c

        lax.fori_loop(0, blocks * n, sent, 0)

        def finish(p, c):
            @pl.when(p != me)
            def _():
                back_copy(p).wait_send()
                pltpu.make_async_remote_copy(
                    src_ref=ret.at[p],
                    dst_ref=back_ref.at[p],
                    send_sem=bsend.at[p],
                    recv_sem=brecv.at[p],
                    device_id={"shots": p},
                    device_id_type=MESH,
                ).wait_recv()

            return c

        lax.fori_loop(0, n, finish, 0)


def inverse_kernel(p_ref, base_ref, o_ref):
    bins, half = p_ref.shape[0], p_ref.shape[-1]
    block = p_ref[...].reshape(bins * 2 * SB, half)
    turned = block.T
    base = base_ref[...]
    mod = row_mod(base.shape)
    for s in range(SB):
        rhs = jnp.where(mod == s, base, jnp.zeros_like(base))
        o_ref[s] = jnp.dot(turned, rhs, preferred_element_type=jnp.float32).astype(jnp.bfloat16)


def fused(records, missing, neighbours, weights, freq_bins):
    n = lax.axis_size("shots")
    rows, order, samples = records.shape
    half = order // 2
    bins = freq_bins.shape[0]
    blocks = rows // SB
    forward, inverse = tables(freq_bins, samples)
    forward = jnp.repeat(forward.reshape(2 * bins, samples), SB, axis=0)
    inverse = jnp.repeat(inverse.reshape(2 * bins, samples), SB, axis=0)
    b = jnp.arange(n // 2, dtype=jnp.int32)
    first = jnp.clip(2 * b - 1, 0, n - 4) * rows
    gshape = (n // 2, 2 * rows, 4 * rows)
    row_ids = (b[:, None] * 2 * rows + jnp.arange(2 * rows, dtype=jnp.int32)[None, :])[:, :, None]
    col_ids = (first[:, None] + jnp.arange(4 * rows, dtype=jnp.int32)[None, :])[:, None, :]
    gb = fill_rows(missing, neighbours, weights, row_ids, col_ids)
    assert gb.shape == gshape
    cut = bins * 2 * SB
    bf16 = jnp.bfloat16
    dma = pltpu.SemaphoreType.DMA
    back = pl.pallas_call(
        functools.partial(main_kernel, n, bins, rows, half, blocks),
        grid=(blocks, 2),
        out_shape=jax.ShapeDtypeStruct((n, 2, rows, half), bf16),
        in_specs=[
            pl.BlockSpec((SB, half, samples), lambda i, j: (i, j, 0)),
            pl.BlockSpec((cut, samples), lambda i, j: (0, 0)),
            pl.BlockSpec(gshape, lambda i, j: (0, 0, 0)),
        ],
        out_specs=pl.BlockSpec(memory_space=pl.ANY),
        scratch_shapes=[
            pltpu.VMEM((bins, 2, 2, rows, half), bf16),
            pltpu.VMEM((n, 2, rows, half), bf16),
            pltpu.VMEM((n, 2, rows, half), bf16),
            pltpu.VMEM((2, 2, order, half), bf16),
            pltpu.VMEM((3, order, half), bf16),
            pltpu.VMEM((n, 2, rows, half), bf16),
            dma((n, blocks)),
            dma((n, blocks)),
            dma((n, blocks)),
            dma((n, blocks)),
            dma((n,)),
            dma((n,)),
            dma,
        ],
        compiler_params=pltpu.CompilerParams(
            collective_id=0, has_side_effects=True, vmem_limit_bytes=50 * 2**20
        ),
    )(records, forward, gb)
    back = back.reshape(bins, 2, 2, rows, half)
    return pl.pallas_call(
        inverse_kernel,
        grid=(blocks, 2),
        out_shape=jax.ShapeDtypeStruct(records.shape, bf16),
        in_specs=[
            pl.BlockSpec((bins, None, 2, SB, half), lambda i, j: (0, j, 0, i, 0)),
            pl.BlockSpec((cut, samples), lambda i, j: (0, 0)),
        ],
        out_specs=pl.BlockSpec((SB, half, samples), lambda i, j: (i, j, 0)),
        compiler_params=pltpu.CompilerParams(vmem_limit_bytes=50 * 2**20),
    )(back, inverse)


def plain(records, missing, neighbours, weights, freq_bins):
    devices = lax.axis_size("shots")
    position = lax.axis_index("shots")
    shot_rows, order, sample_count = records.shape
    half = order // 2
    couples = devices // 2
    forward, inverse = tables(freq_bins, sample_count)
    blocked = records.reshape(shot_rows, 2, half, sample_count)
    spectra = jnp.einsum(
        "shrt,pct->phcsr", blocked, forward, preferred_element_type=jnp.float32
    ).astype(jnp.bfloat16)
    outgoing = spectra.reshape(devices, 2, shot_rows, half)
    own = lax.all_to_all(outgoing, "shots", split_axis=0, concat_axis=2, tiled=True)[0]
    ids = jnp.arange(order, dtype=jnp.int32)
    g = fill_rows(missing, neighbours, weights, ids[:, None], ids[None, :])
    own = jnp.einsum("st,ctr->csr", g, own, preferred_element_type=jnp.float32)
    own = own.astype(jnp.bfloat16)
    member = position % 2
    other = lax.ppermute(own, "shots", [(i, i ^ 1) for i in range(devices)])
    real, imag = 0.0, 0.0
    for left, part in ((own, member), (other, 1 - member)):
        right = lax.dynamic_slice_in_dim(own, part * half, half, 1)
        dot = functools.partial(jnp.dot, preferred_element_type=jnp.float32)
        real = real + dot(left[0], right[0]) - dot(left[1], right[1])
        imag = imag + dot(left[0], right[1]) + dot(left[1], right[0])
    predicted = (jnp.stack([real, imag]) * (-1.0 / math.sqrt(order))).astype(jnp.bfloat16)
    outgoing = predicted.reshape(2, devices, shot_rows, half)
    outgoing = jnp.transpose(outgoing, (1, 0, 2, 3))
    returned = lax.all_to_all(outgoing, "shots", split_axis=0, concat_axis=0, tiled=True)
    returned = returned.reshape(couples, 2, 2, shot_rows, half)
    multiples = jnp.einsum(
        "phcsr,pct->shrt", returned, inverse, preferred_element_type=jnp.float32
    )
    return multiples.astype(jnp.bfloat16).reshape(shot_rows, order, sample_count)


def shards(records, missing, neighbours, weights, freq_bins):
    n = lax.axis_size("shots")
    rows, order, samples = records.shape
    bins = freq_bins.shape[0]
    fits = (
        rows % SB == 0 and n % 4 == 0 and n >= 8 and n == 2 * bins and order == n * rows
        and order % 512 == 0 and rows >= 2 and bins <= 8
    )
    return (fused if fits else plain)(records, missing, neighbours, weights, freq_bins)


def solution(mesh):
    return jax.shard_map(
        shards,
        mesh=mesh,
        in_specs=(
            P(("lines", "shots"), None, None),
            P("lines"),
            P("lines", None),
            P("lines", None),
            P(),
        ),
        out_specs=P(("lines", "shots"), None, None),
        check_vma=False,
    )
```

```python
import functools
import math

import jax
import jax.numpy as jnp
from jax import lax
from jax.experimental import pallas as pl
from jax.experimental.pallas import tpu as pltpu
from jax.sharding import PartitionSpec as P

SB = 16
MESH = pl.DeviceIdType.MESH


def angles_of(freq_bins, sample_count):
    sample_ids = jnp.arange(sample_count, dtype=jnp.int32)
    phases = freq_bins[:, None] * sample_ids[None, :] % sample_count
    angles = phases.astype(jnp.float32) * (2.0 * math.pi / sample_count)
    return jnp.stack([jnp.cos(angles), -jnp.sin(angles)], axis=1)


def tables(freq_bins, sample_count):
    trig_pair = angles_of(freq_bins, sample_count)
    forward = (trig_pair / math.sqrt(sample_count)).astype(jnp.bfloat16)
    inverse = (trig_pair * math.sqrt(2.0 / freq_bins.shape[0])).astype(jnp.bfloat16)
    return (forward, inverse)


def fill_rows(missing, neighbours, weights, rows, cols):
    hit = missing[None, :] == rows.reshape(-1, 1)
    kept = jnp.logical_not(jnp.any(hit, axis=1)).reshape(rows.shape)
    out = jnp.where((rows == cols) & kept, 1.0, 0.0)
    for k in range(neighbours.shape[1]):
        w = jnp.sum(jnp.where(hit, weights[None, :, k], 0.0), axis=1).reshape(rows.shape)
        n = jnp.sum(jnp.where(hit, neighbours[None, :, k], 0), axis=1).reshape(rows.shape)
        out = out + jnp.where(n == cols, w, 0.0)
    return out.astype(jnp.bfloat16)


def spread(trig):
    count, samples = trig.shape
    wide = jnp.broadcast_to(trig[:, None, :], (count, SB, samples))
    return wide.reshape(count * SB, samples).astype(jnp.bfloat16)


def row_mod(shape):
    return lax.broadcasted_iota(jnp.int32, shape, 0) % SB


def main_kernel(
    n, bins, rows, half, blocks,
    x_ref, trig_ref, miss_ref, neigh_ref, weight_ref, back_ref,
    send, recv, other, full, right, ret, base_ref, gb_ref,
    send_sem, recv_sem, fsend, frecv, bsend, brecv, lsem,
):
    step = pl.program_id(0) * 2 + pl.program_id(1)
    sb, h = pl.program_id(0), pl.program_id(1)
    me = lax.axis_index("shots")
    member = me % 2
    mine = me // 2
    order = n * rows

    @pl.when(step == 0)
    def _():
        barrier = pltpu.get_barrier_semaphore()

        def greet(d, c):
            pl.semaphore_signal(
                barrier, inc=1, device_id={"shots": (me + d) % n}, device_id_type=MESH
            )
            return c

        lax.fori_loop(1, n, greet, 0)
        pl.semaphore_wait(barrier, n - 1)

    samples = x_ref.shape[2]

    @pl.when(step == 0)
    def _():
        base_ref[...] = spread(trig_ref[...] / math.sqrt(samples))

    mod = row_mod((bins * 2 * SB, samples))
    base = base_ref[...]
    acc = jnp.zeros((bins * 2 * SB, half), jnp.float32)
    for s in range(SB):
        left = jnp.where(mod == s, base, jnp.zeros_like(base))
        acc = acc + lax.dot_general(
            left, x_ref[s], (((1,), (1,)), ((), ())), preferred_element_type=jnp.float32
        )
    at = pl.multiple_of(sb * SB, SB)
    send[:, h, :, pl.ds(at, SB), :] = acc.astype(jnp.bfloat16).reshape(bins, 2, SB, half)

    def out_copy(j, hh, sbb):
        a = pl.multiple_of(sbb * SB, SB)
        return pltpu.make_async_remote_copy(
            src_ref=send.at[j, hh, :, pl.ds(a, SB), :],
            dst_ref=recv.at[me, :, pl.ds(a, SB), :],
            send_sem=send_sem.at[j * 2 + hh, sbb],
            recv_sem=recv_sem.at[me, sbb],
            device_id={"shots": j * 2 + hh},
            device_id_type=MESH,
        )

    def start_out(d, c):
        hb = bins // 2
        side = (mine // hb + 1 + d // hb) % 2
        j = side * hb + (mine + 1 + d) % hb

        @pl.when(j * 2 + h != me)
        def _():
            out_copy(j, h, sb).start()

        return c

    lax.fori_loop(0, bins, start_out, 0)

    @pl.when(h == member)
    def _():
        recv[me, :, pl.ds(at, SB), :] = send[mine, h, :, pl.ds(at, SB), :]

    @pl.when(step == 2 * blocks - 1)
    def _():
        sibling = mine * 2 + 1 - member
        miss = miss_ref[...]
        count = miss.shape[1]

        def band(b, c):
            first = jnp.minimum(jnp.maximum(2 * b - 1, 0), n - 4) * rows
            hit = miss == lax.broadcasted_iota(jnp.int32, (2 * rows, count), 0) + b * 2 * rows
            hit = jnp.where(hit, 1.0, 0.0)
            kept = 1.0 - jnp.sum(hit, axis=1, keepdims=True)
            cols = lax.broadcasted_iota(jnp.int32, (count, 4 * rows), 1) + first
            near = jnp.zeros((count, 4 * rows), jnp.float32)
            for k in range(neigh_ref.shape[1]):
                near = near + jnp.where(
                    neigh_ref[:, k:k + 1] == cols, weight_ref[:, k:k + 1], 0.0
                )
            row_id = lax.broadcasted_iota(jnp.int32, (2 * rows, 4 * rows), 0) + b * 2 * rows
            col_id = lax.broadcasted_iota(jnp.int32, (2 * rows, 4 * rows), 1) + first
            g = jnp.dot(
                hit.astype(jnp.bfloat16),
                near.astype(jnp.bfloat16),
                preferred_element_type=jnp.float32,
            ) + jnp.where(row_id == col_id, kept, 0.0)
            gb_ref[b] = g.astype(jnp.bfloat16)
            return c

        lax.fori_loop(0, n // 2, band, 0)

        def forward(p, sbb):
            a = pl.multiple_of(sbb * SB, SB)
            return pltpu.make_async_remote_copy(
                src_ref=recv.at[p, :, pl.ds(a, SB), :],
                dst_ref=other.at[p, :, pl.ds(a, SB), :],
                send_sem=fsend.at[p, sbb],
                recv_sem=frecv.at[p, sbb],
                device_id={"shots": sibling},
                device_id_type=MESH,
            )

        def arrive(i, c):
            sbb, p = i // n, (me + i) % n
            a = pl.multiple_of(sbb * SB, SB)

            @pl.when(p != me)
            def _():
                pltpu.make_async_remote_copy(
                    src_ref=recv.at[p, :, pl.ds(a, SB), :],
                    dst_ref=recv.at[p, :, pl.ds(a, SB), :],
                    send_sem=send_sem.at[p, sbb],
                    recv_sem=recv_sem.at[p, sbb],
                    device_id={"shots": sibling},
                    device_id_type=MESH,
                ).wait_recv()

            forward(p, sbb).start()
            return c

        lax.fori_loop(0, blocks * n, arrive, 0)

        def fill(src, keep, low, high):
            def one(b, c):
                first = jnp.minimum(jnp.maximum(2 * b - 1, 0), n - 4)
                g = gb_ref[b]
                at_row = pl.multiple_of(b * 2 * rows, 2 * rows)
                for ch in range(2):
                    piece = src[pl.ds(first, 4), ch].reshape(4 * rows, half)
                    val = jnp.dot(g, piece, preferred_element_type=jnp.float32)
                    keep(ch, at_row, val.astype(jnp.bfloat16))
                return c

            lax.fori_loop(low, high, one, 0)

        def keep_own(ch, at_row, val):
            full[ch, member, pl.ds(at_row, 2 * rows), :] = val
            right[ch, pl.ds(at_row, 2 * rows), :] = val
            if ch == 1:
                right[2, pl.ds(at_row, 2 * rows), :] = -val

        def keep_other(ch, at_row, val):
            full[ch, 1 - member, pl.ds(at_row, 2 * rows), :] = val

        fill(recv, keep_own, 0, n // 2)

        def arrived(i, c):
            forward(i % n, i // n).wait()
            return c

        lax.fori_loop(0, blocks * n, arrived, 0)

        def back_copy(p):
            return pltpu.make_async_remote_copy(
                src_ref=ret.at[p],
                dst_ref=back_ref.at[me],
                send_sem=bsend.at[p],
                recv_sem=brecv.at[me],
                device_id={"shots": p},
                device_id_type=MESH,
            )

        own_back = pltpu.make_async_copy(ret.at[me], back_ref.at[me], lsem)
        factor = -1.0 / math.sqrt(order)
        groups = n // 4
        wide = 256

        def product(i, c):
            hg = groups // 2
            z = me // 4
            g = (z // hg + 1 + i // hg) % 2 * hg + (z + 1 + i) % hg
            at_row = pl.multiple_of(g * 4 * rows, 4 * rows)
            fill(other, keep_other, 2 * g, 2 * g + 2)

            for col in range(0, half, wide):
                for ch in range(2):
                    out = None
                    for m in range(2):
                        for lc in range(2):
                            rc = (0 if lc == 0 else 2) if ch == 0 else (1 if lc == 0 else 0)
                            term = jnp.dot(
                                full[lc, m, pl.ds(at_row, 4 * rows), :],
                                right[rc, m * half:(m + 1) * half, col:col + wide],
                                preferred_element_type=jnp.float32,
                            )
                            out = term if out is None else out + term
                    ret[pl.ds(4 * g, 4), ch, :, col:col + wide] = (
                        (out * factor).astype(jnp.bfloat16).reshape(4, rows, wide)
                    )

            def post(q, c2):
                p = 4 * g + q

                @pl.when(p != me)
                def _():
                    back_copy(p).start()

                @pl.when(p == me)
                def _():
                    own_back.start()

                return c2

            lax.fori_loop(0, 4, post, 0)
            return c

        lax.fori_loop(0, groups, product, 0)
        own_back.wait()

        def sent(i, c):
            sbb, p = i // n, i % n

            @pl.when(p != me)
            def _():
                out_copy(p // 2, p % 2, sbb).wait_send()

            return c

        lax.fori_loop(0, blocks * n, sent, 0)

        def finish(p, c):
            @pl.when(p != me)
            def _():
                back_copy(p).wait_send()
                pltpu.make_async_remote_copy(
                    src_ref=ret.at[p],
                    dst_ref=back_ref.at[p],
                    send_sem=bsend.at[p],
                    recv_sem=brecv.at[p],
                    device_id={"shots": p},
                    device_id_type=MESH,
                ).wait_recv()

            return c

        lax.fori_loop(0, n, finish, 0)


def inverse_kernel(p_ref, trig_ref, o_ref, base_ref):
    @pl.when((pl.program_id(0) == 0) & (pl.program_id(1) == 0))
    def _():
        base_ref[...] = spread(trig_ref[...] * math.sqrt(2.0 / p_ref.shape[0]))

    bins, half = p_ref.shape[0], p_ref.shape[-1]
    block = p_ref[...].reshape(bins * 2 * SB, half)
    turned = block.T
    base = base_ref[...]
    mod = row_mod(base.shape)
    for s in range(SB):
        rhs = jnp.where(mod == s, base, jnp.zeros_like(base))
        o_ref[s] = jnp.dot(turned, rhs, preferred_element_type=jnp.float32).astype(jnp.bfloat16)


def fused(records, missing, neighbours, weights, freq_bins):
    n = lax.axis_size("shots")
    rows, order, samples = records.shape
    half = order // 2
    bins = freq_bins.shape[0]
    blocks = rows // SB
    trig = angles_of(freq_bins, samples).reshape(2 * bins, samples)
    count = missing.shape[0]
    gshape = (n // 2, 2 * rows, 4 * rows)
    cut = bins * 2 * SB
    bf16 = jnp.bfloat16
    dma = pltpu.SemaphoreType.DMA
    back = pl.pallas_call(
        functools.partial(main_kernel, n, bins, rows, half, blocks),
        grid=(blocks, 2),
        out_shape=jax.ShapeDtypeStruct((n, 2, rows, half), bf16),
        in_specs=[
            pl.BlockSpec((SB, half, samples), lambda i, j: (i, j, 0)),
            pl.BlockSpec((2 * bins, samples), lambda i, j: (0, 0)),
            pl.BlockSpec((1, count), lambda i, j: (0, 0)),
            pl.BlockSpec(neighbours.shape, lambda i, j: (0, 0)),
            pl.BlockSpec(weights.shape, lambda i, j: (0, 0)),
        ],
        out_specs=pl.BlockSpec(memory_space=pl.ANY),
        scratch_shapes=[
            pltpu.VMEM((bins, 2, 2, rows, half), bf16),
            pltpu.VMEM((n, 2, rows, half), bf16),
            pltpu.VMEM((n, 2, rows, half), bf16),
            pltpu.VMEM((2, 2, order, half), bf16),
            pltpu.VMEM((3, order, half), bf16),
            pltpu.VMEM((n, 2, rows, half), bf16),
            pltpu.VMEM((cut, samples), bf16),
            pltpu.VMEM(gshape, bf16),
            dma((n, blocks)),
            dma((n, blocks)),
            dma((n, blocks)),
            dma((n, blocks)),
            dma((n,)),
            dma((n,)),
            dma,
        ],
        compiler_params=pltpu.CompilerParams(
            collective_id=0, has_side_effects=True, vmem_limit_bytes=50 * 2**20
        ),
    )(records, trig, missing.reshape(1, count), neighbours, weights)
    back = back.reshape(bins, 2, 2, rows, half)
    return pl.pallas_call(
        inverse_kernel,
        grid=(blocks, 2),
        out_shape=jax.ShapeDtypeStruct(records.shape, bf16),
        in_specs=[
            pl.BlockSpec((bins, None, 2, SB, half), lambda i, j: (0, j, 0, i, 0)),
            pl.BlockSpec((2 * bins, samples), lambda i, j: (0, 0)),
        ],
        scratch_shapes=[pltpu.VMEM((cut, samples), bf16)],
        out_specs=pl.BlockSpec((SB, half, samples), lambda i, j: (i, j, 0)),
        compiler_params=pltpu.CompilerParams(vmem_limit_bytes=50 * 2**20),
    )(back, trig)


def plain(records, missing, neighbours, weights, freq_bins):
    devices = lax.axis_size("shots")
    position = lax.axis_index("shots")
    shot_rows, order, sample_count = records.shape
    half = order // 2
    couples = devices // 2
    forward, inverse = tables(freq_bins, sample_count)
    blocked = records.reshape(shot_rows, 2, half, sample_count)
    spectra = jnp.einsum(
        "shrt,pct->phcsr", blocked, forward, preferred_element_type=jnp.float32
    ).astype(jnp.bfloat16)
    outgoing = spectra.reshape(devices, 2, shot_rows, half)
    own = lax.all_to_all(outgoing, "shots", split_axis=0, concat_axis=2, tiled=True)[0]
    ids = jnp.arange(order, dtype=jnp.int32)
    g = fill_rows(missing, neighbours, weights, ids[:, None], ids[None, :])
    own = jnp.einsum("st,ctr->csr", g, own, preferred_element_type=jnp.float32)
    own = own.astype(jnp.bfloat16)
    member = position % 2
    other = lax.ppermute(own, "shots", [(i, i ^ 1) for i in range(devices)])
    real, imag = 0.0, 0.0
    for left, part in ((own, member), (other, 1 - member)):
        right = lax.dynamic_slice_in_dim(own, part * half, half, 1)
        dot = functools.partial(jnp.dot, preferred_element_type=jnp.float32)
        real = real + dot(left[0], right[0]) - dot(left[1], right[1])
        imag = imag + dot(left[0], right[1]) + dot(left[1], right[0])
    predicted = (jnp.stack([real, imag]) * (-1.0 / math.sqrt(order))).astype(jnp.bfloat16)
    outgoing = predicted.reshape(2, devices, shot_rows, half)
    outgoing = jnp.transpose(outgoing, (1, 0, 2, 3))
    returned = lax.all_to_all(outgoing, "shots", split_axis=0, concat_axis=0, tiled=True)
    returned = returned.reshape(couples, 2, 2, shot_rows, half)
    multiples = jnp.einsum(
        "phcsr,pct->shrt", returned, inverse, preferred_element_type=jnp.float32
    )
    return multiples.astype(jnp.bfloat16).reshape(shot_rows, order, sample_count)


def shards(records, missing, neighbours, weights, freq_bins):
    n = lax.axis_size("shots")
    rows, order, samples = records.shape
    bins = freq_bins.shape[0]
    fits = (
        rows % SB == 0 and n % 4 == 0 and n >= 8 and n == 2 * bins and order == n * rows
        and order % 512 == 0 and rows >= 2 and bins <= 8
    )
    return (fused if fits else plain)(records, missing, neighbours, weights, freq_bins)


def solution(mesh):
    return jax.shard_map(
        shards,
        mesh=mesh,
        in_specs=(
            P(("lines", "shots"), None, None),
            P("lines"),
            P("lines", None),
            P("lines", None),
            P(),
        ),
        out_specs=P(("lines", "shots"), None, None),
        check_vma=False,
    )
```

```python
import functools
import math

import jax
import jax.numpy as jnp
from jax import lax
from jax.experimental import pallas as pl
from jax.experimental.pallas import tpu as pltpu
from jax.sharding import PartitionSpec as P

SB = 16
MESH = pl.DeviceIdType.MESH


def angles_of(freq_bins, sample_count):
    sample_ids = jnp.arange(sample_count, dtype=jnp.int32)
    phases = freq_bins[:, None] * sample_ids[None, :] % sample_count
    angles = phases.astype(jnp.float32) * (2.0 * math.pi / sample_count)
    return jnp.stack([jnp.cos(angles), -jnp.sin(angles)], axis=1)


def tables(freq_bins, sample_count):
    trig_pair = angles_of(freq_bins, sample_count)
    forward = (trig_pair / math.sqrt(sample_count)).astype(jnp.bfloat16)
    inverse = (trig_pair * math.sqrt(2.0 / freq_bins.shape[0])).astype(jnp.bfloat16)
    return (forward, inverse)


def fill_rows(missing, neighbours, weights, rows, cols):
    hit = missing[None, :] == rows.reshape(-1, 1)
    kept = jnp.logical_not(jnp.any(hit, axis=1)).reshape(rows.shape)
    out = jnp.where((rows == cols) & kept, 1.0, 0.0)
    for k in range(neighbours.shape[1]):
        w = jnp.sum(jnp.where(hit, weights[None, :, k], 0.0), axis=1).reshape(rows.shape)
        n = jnp.sum(jnp.where(hit, neighbours[None, :, k], 0), axis=1).reshape(rows.shape)
        out = out + jnp.where(n == cols, w, 0.0)
    return out.astype(jnp.bfloat16)


def spread(trig):
    count, samples = trig.shape
    wide = jnp.broadcast_to(trig[:, None, :], (count, SB, samples))
    return wide.reshape(count * SB, samples).astype(jnp.bfloat16)


def row_mod(shape):
    return lax.broadcasted_iota(jnp.int32, shape, 0) % SB


def main_kernel(
    n, bins, rows, half, blocks,
    x_ref, trig_ref, miss_ref, neigh_ref, weight_ref, back_ref,
    send, recv, other, full, right, ret, base_ref, gb_ref,
    send_sem, recv_sem, fsend, frecv, bsend, brecv, lsem,
):
    step = pl.program_id(0) * 2 + pl.program_id(1)
    sb, h = pl.program_id(0), pl.program_id(1)
    me = lax.axis_index("shots")
    member = me % 2
    mine = me // 2
    order = n * rows

    @pl.when(step == 0)
    def _():
        barrier = pltpu.get_barrier_semaphore()

        def greet(d, c):
            pl.semaphore_signal(
                barrier, inc=1, device_id={"shots": (me + d) % n}, device_id_type=MESH
            )
            return c

        lax.fori_loop(1, n, greet, 0)
        pl.semaphore_wait(barrier, n - 1)

    samples = x_ref.shape[2]

    @pl.when(step == 0)
    def _():
        base_ref[...] = spread(trig_ref[...] / math.sqrt(samples))

    mod = row_mod((bins * 2 * SB, samples))
    base = base_ref[...]
    acc = jnp.zeros((bins * 2 * SB, half), jnp.float32)
    for s in range(SB):
        left = jnp.where(mod == s, base, jnp.zeros_like(base))
        acc = acc + lax.dot_general(
            left, x_ref[s], (((1,), (1,)), ((), ())), preferred_element_type=jnp.float32
        )
    at = pl.multiple_of(sb * SB, SB)
    send[:, h, :, pl.ds(at, SB), :] = acc.astype(jnp.bfloat16).reshape(bins, 2, SB, half)

    def out_copy(j, hh, sbb):
        a = pl.multiple_of(sbb * SB, SB)
        return pltpu.make_async_remote_copy(
            src_ref=send.at[j, hh, :, pl.ds(a, SB), :],
            dst_ref=recv.at[me, :, pl.ds(a, SB), :],
            send_sem=send_sem.at[j * 2 + hh, sbb],
            recv_sem=recv_sem.at[me, sbb],
            device_id={"shots": j * 2 + hh},
            device_id_type=MESH,
        )

    def start_out(d, c):
        j = (mine + 1 + d) % bins

        @pl.when(j * 2 + h != me)
        def _():
            out_copy(j, h, sb).start()

        return c

    lax.fori_loop(0, bins, start_out, 0)

    @pl.when(h == member)
    def _():
        recv[me, :, pl.ds(at, SB), :] = send[mine, h, :, pl.ds(at, SB), :]

    @pl.when(step == 2 * blocks - 1)
    def _():
        sibling = mine * 2 + 1 - member
        miss = miss_ref[...]
        count = miss.shape[1]

        def band(b, c):
            first = jnp.minimum(jnp.maximum(2 * b - 1, 0), n - 4) * rows
            hit = miss == lax.broadcasted_iota(jnp.int32, (2 * rows, count), 0) + b * 2 * rows
            hit = jnp.where(hit, 1.0, 0.0)
            kept = 1.0 - jnp.sum(hit, axis=1, keepdims=True)
            cols = lax.broadcasted_iota(jnp.int32, (4 * rows, count), 0) + first
            near = jnp.zeros((4 * rows, count), jnp.float32)
            for k in range(neigh_ref.shape[0]):
                near = near + jnp.where(
                    neigh_ref[k:k + 1, :] == cols, weight_ref[k:k + 1, :], 0.0
                )
            row_id = lax.broadcasted_iota(jnp.int32, (2 * rows, 4 * rows), 0) + b * 2 * rows
            col_id = lax.broadcasted_iota(jnp.int32, (2 * rows, 4 * rows), 1) + first
            g = lax.dot_general(
                hit.astype(jnp.bfloat16),
                near.astype(jnp.bfloat16),
                (((1,), (1,)), ((), ())),
                preferred_element_type=jnp.float32,
            ) + jnp.where(row_id == col_id, kept, 0.0)
            gb_ref[b] = g.astype(jnp.bfloat16)
            return c

        lax.fori_loop(0, n // 2, band, 0)

        def forward(p, sbb):
            a = pl.multiple_of(sbb * SB, SB)
            return pltpu.make_async_remote_copy(
                src_ref=recv.at[p, :, pl.ds(a, SB), :],
                dst_ref=other.at[p, :, pl.ds(a, SB), :],
                send_sem=fsend.at[p, sbb],
                recv_sem=frecv.at[p, sbb],
                device_id={"shots": sibling},
                device_id_type=MESH,
            )

        def arrive(i, c):
            sbb, p = i // n, (me + i) % n
            a = pl.multiple_of(sbb * SB, SB)

            @pl.when(p != me)
            def _():
                pltpu.make_async_remote_copy(
                    src_ref=recv.at[p, :, pl.ds(a, SB), :],
                    dst_ref=recv.at[p, :, pl.ds(a, SB), :],
                    send_sem=send_sem.at[p, sbb],
                    recv_sem=recv_sem.at[p, sbb],
                    device_id={"shots": sibling},
                    device_id_type=MESH,
                ).wait_recv()

            forward(p, sbb).start()
            return c

        lax.fori_loop(0, blocks * n, arrive, 0)

        def fill(src, keep, low, high):
            def one(b, c):
                first = jnp.minimum(jnp.maximum(2 * b - 1, 0), n - 4)
                g = gb_ref[b]
                at_row = pl.multiple_of(b * 2 * rows, 2 * rows)
                for ch in range(2):
                    piece = src[pl.ds(first, 4), ch].reshape(4 * rows, half)
                    val = jnp.dot(g, piece, preferred_element_type=jnp.float32)
                    keep(ch, at_row, val.astype(jnp.bfloat16))
                return c

            lax.fori_loop(low, high, one, 0)

        def keep_own(ch, at_row, val):
            full[ch, member, pl.ds(at_row, 2 * rows), :] = val
            right[ch, pl.ds(at_row, 2 * rows), :] = val
            if ch == 1:
                right[2, pl.ds(at_row, 2 * rows), :] = -val

        def keep_other(ch, at_row, val):
            full[ch, 1 - member, pl.ds(at_row, 2 * rows), :] = val

        fill(recv, keep_own, 0, n // 2)

        def arrived(i, c):
            forward(i % n, i // n).wait()
            return c

        lax.fori_loop(0, blocks * n, arrived, 0)

        def back_copy(p):
            return pltpu.make_async_remote_copy(
                src_ref=ret.at[p],
                dst_ref=back_ref.at[me],
                send_sem=bsend.at[p],
                recv_sem=brecv.at[me],
                device_id={"shots": p},
                device_id_type=MESH,
            )

        own_back = pltpu.make_async_copy(ret.at[me], back_ref.at[me], lsem)
        factor = -1.0 / math.sqrt(order)
        groups = n // 4
        wide = 256

        def product(i, c):
            g = (me // 4 + groups // 2 + i) % groups
            at_row = pl.multiple_of(g * 4 * rows, 4 * rows)
            fill(other, keep_other, 2 * g, 2 * g + 2)

            for col in range(0, half, wide):
                for ch in range(2):
                    out = None
                    for m in range(2):
                        for lc in range(2):
                            rc = (0 if lc == 0 else 2) if ch == 0 else (1 if lc == 0 else 0)
                            term = jnp.dot(
                                full[lc, m, pl.ds(at_row, 4 * rows), :],
                                right[rc, m * half:(m + 1) * half, col:col + wide],
                                preferred_element_type=jnp.float32,
                            )
                            out = term if out is None else out + term
                    ret[pl.ds(4 * g, 4), ch, :, col:col + wide] = (
                        (out * factor).astype(jnp.bfloat16).reshape(4, rows, wide)
                    )

            def post(q, c2):
                p = 4 * g + q

                @pl.when(p != me)
                def _():
                    back_copy(p).start()

                @pl.when(p == me)
                def _():
                    own_back.start()

                return c2

            lax.fori_loop(0, 4, post, 0)
            return c

        lax.fori_loop(0, groups, product, 0)
        own_back.wait()

        def sent(i, c):
            sbb, p = i // n, i % n

            @pl.when(p != me)
            def _():
                out_copy(p // 2, p % 2, sbb).wait_send()

            return c

        lax.fori_loop(0, blocks * n, sent, 0)

        def finish(p, c):
            @pl.when(p != me)
            def _():
                back_copy(p).wait_send()
                pltpu.make_async_remote_copy(
                    src_ref=ret.at[p],
                    dst_ref=back_ref.at[p],
                    send_sem=bsend.at[p],
                    recv_sem=brecv.at[p],
                    device_id={"shots": p},
                    device_id_type=MESH,
                ).wait_recv()

            return c

        lax.fori_loop(0, n, finish, 0)


def inverse_kernel(p_ref, trig_ref, o_ref, base_ref):
    @pl.when((pl.program_id(0) == 0) & (pl.program_id(1) == 0))
    def _():
        base_ref[...] = spread(trig_ref[...] * math.sqrt(2.0 / p_ref.shape[0]))

    bins, half = p_ref.shape[0], p_ref.shape[-1]
    block = p_ref[...].reshape(bins * 2 * SB, half)
    turned = block.T
    base = base_ref[...]
    mod = row_mod(base.shape)
    for s in range(SB):
        rhs = jnp.where(mod == s, base, jnp.zeros_like(base))
        o_ref[s] = jnp.dot(turned, rhs, preferred_element_type=jnp.float32).astype(jnp.bfloat16)


def fused(records, missing, neighbours, weights, freq_bins):
    n = lax.axis_size("shots")
    rows, order, samples = records.shape
    half = order // 2
    bins = freq_bins.shape[0]
    blocks = rows // SB
    trig = angles_of(freq_bins, samples).reshape(2 * bins, samples)
    count = missing.shape[0]
    gshape = (n // 2, 2 * rows, 4 * rows)
    cut = bins * 2 * SB
    bf16 = jnp.bfloat16
    dma = pltpu.SemaphoreType.DMA
    back = pl.pallas_call(
        functools.partial(main_kernel, n, bins, rows, half, blocks),
        grid=(blocks, 2),
        out_shape=jax.ShapeDtypeStruct((n, 2, rows, half), bf16),
        in_specs=[
            pl.BlockSpec((SB, half, samples), lambda i, j: (i, j, 0)),
            pl.BlockSpec((2 * bins, samples), lambda i, j: (0, 0)),
            pl.BlockSpec((1, count), lambda i, j: (0, 0)),
            pl.BlockSpec(neighbours.shape[::-1], lambda i, j: (0, 0)),
            pl.BlockSpec(weights.shape[::-1], lambda i, j: (0, 0)),
        ],
        out_specs=pl.BlockSpec(memory_space=pl.ANY),
        scratch_shapes=[
            pltpu.VMEM((bins, 2, 2, rows, half), bf16),
            pltpu.VMEM((n, 2, rows, half), bf16),
            pltpu.VMEM((n, 2, rows, half), bf16),
            pltpu.VMEM((2, 2, order, half), bf16),
            pltpu.VMEM((3, order, half), bf16),
            pltpu.VMEM((n, 2, rows, half), bf16),
            pltpu.VMEM((cut, samples), bf16),
            pltpu.VMEM(gshape, bf16),
            dma((n, blocks)),
            dma((n, blocks)),
            dma((n, blocks)),
            dma((n, blocks)),
            dma((n,)),
            dma((n,)),
            dma,
        ],
        compiler_params=pltpu.CompilerParams(
            collective_id=0, has_side_effects=True, vmem_limit_bytes=50 * 2**20
        ),
    )(records, trig, missing.reshape(1, count), neighbours.T, weights.T)
    back = back.reshape(bins, 2, 2, rows, half)
    return pl.pallas_call(
        inverse_kernel,
        grid=(blocks, 2),
        out_shape=jax.ShapeDtypeStruct(records.shape, bf16),
        in_specs=[
            pl.BlockSpec((bins, None, 2, SB, half), lambda i, j: (0, j, 0, i, 0)),
            pl.BlockSpec((2 * bins, samples), lambda i, j: (0, 0)),
        ],
        scratch_shapes=[pltpu.VMEM((cut, samples), bf16)],
        out_specs=pl.BlockSpec((SB, half, samples), lambda i, j: (i, j, 0)),
        compiler_params=pltpu.CompilerParams(vmem_limit_bytes=50 * 2**20),
    )(back, trig)


def plain(records, missing, neighbours, weights, freq_bins):
    devices = lax.axis_size("shots")
    position = lax.axis_index("shots")
    shot_rows, order, sample_count = records.shape
    half = order // 2
    couples = devices // 2
    forward, inverse = tables(freq_bins, sample_count)
    blocked = records.reshape(shot_rows, 2, half, sample_count)
    spectra = jnp.einsum(
        "shrt,pct->phcsr", blocked, forward, preferred_element_type=jnp.float32
    ).astype(jnp.bfloat16)
    outgoing = spectra.reshape(devices, 2, shot_rows, half)
    own = lax.all_to_all(outgoing, "shots", split_axis=0, concat_axis=2, tiled=True)[0]
    ids = jnp.arange(order, dtype=jnp.int32)
    g = fill_rows(missing, neighbours, weights, ids[:, None], ids[None, :])
    own = jnp.einsum("st,ctr->csr", g, own, preferred_element_type=jnp.float32)
    own = own.astype(jnp.bfloat16)
    member = position % 2
    other = lax.ppermute(own, "shots", [(i, i ^ 1) for i in range(devices)])
    real, imag = 0.0, 0.0
    for left, part in ((own, member), (other, 1 - member)):
        right = lax.dynamic_slice_in_dim(own, part * half, half, 1)
        dot = functools.partial(jnp.dot, preferred_element_type=jnp.float32)
        real = real + dot(left[0], right[0]) - dot(left[1], right[1])
        imag = imag + dot(left[0], right[1]) + dot(left[1], right[0])
    predicted = (jnp.stack([real, imag]) * (-1.0 / math.sqrt(order))).astype(jnp.bfloat16)
    outgoing = predicted.reshape(2, devices, shot_rows, half)
    outgoing = jnp.transpose(outgoing, (1, 0, 2, 3))
    returned = lax.all_to_all(outgoing, "shots", split_axis=0, concat_axis=0, tiled=True)
    returned = returned.reshape(couples, 2, 2, shot_rows, half)
    multiples = jnp.einsum(
        "phcsr,pct->shrt", returned, inverse, preferred_element_type=jnp.float32
    )
    return multiples.astype(jnp.bfloat16).reshape(shot_rows, order, sample_count)


def shards(records, missing, neighbours, weights, freq_bins):
    n = lax.axis_size("shots")
    rows, order, samples = records.shape
    bins = freq_bins.shape[0]
    fits = (
        rows % SB == 0 and n % 4 == 0 and n >= 8 and n == 2 * bins and order == n * rows
        and order % 512 == 0 and rows >= 2 and bins <= 8
    )
    return (fused if fits else plain)(records, missing, neighbours, weights, freq_bins)


def solution(mesh):
    return jax.shard_map(
        shards,
        mesh=mesh,
        in_specs=(
            P(("lines", "shots"), None, None),
            P("lines"),
            P("lines", None),
            P("lines", None),
            P(),
        ),
        out_specs=P(("lines", "shots"), None, None),
        check_vma=False,
    )
```
